32 devices in a mesh: groups: 2 (over x), ctx: 16 (over z, y, core).
Axes of the slice: x: 2, y: 2, z: 4, core: 2. Of those that a mesh axis runs over, the one named last changes fastest.
Arguments:
- hidden: bfloat16 [16384, 1024], P(('groups', 'ctx')), parts along dimension 0, may hold values from -6 to 6
- query_weight: bfloat16 [1024, 1024], replicated, may hold values from -0.1875 to 0.1875
- key_weight: bfloat16 [1024, 1024], replicated, may hold values from -0.1875 to 0.1875
- value_weight: bfloat16 [1024, 1024], replicated, may hold values from -0.1875 to 0.1875
- output_weight: bfloat16 [1024, 1024], replicated, may hold values from -0.1875 to 0.1875
- decay_log: float32 [16384, 8], P(('groups', 'ctx')), parts along dimension 0, may hold values from -1 to 0, as said below
- doc_starts: int32 [8], P('groups'), parts along dimension 0, may hold values from 0 to 8128, as said below
Outputs:
- mixed: bfloat16 [16384, 1024], P(('groups', 'ctx')), parts along dimension 0
The draws below stay inside these ranges and needn't reach their ends.
There are 2 independent parts, one for each index of `groups`. The reference program is written for one: setup_inputs(seed, part) draws one part's arguments, and reference() takes and returns one part's arrays. A program takes and returns all parts, laid end to end along the dimension named above; an argument that names none is the same for every part. Nothing has to cross between parts.
Inputs may be any that keep to these rules, and one draw needn't show every extreme that they name: Every entry of decay_log is negative. doc_starts is non-decreasing, its first entry is 0, its last entry is 8128, and every entry is a multiple of 64; a repeated entry marks an empty document.
All inputs are finite; a program needn't handle non-finite values.
Results may differ from the reference program's by a relative error of at most 0.0069.
Values sent between devices are 32-bit elements; how exact they have to be, the bound alone decides.
A program may use at most 192 MiB of HBM per device.

```python
import math
import jax
import jax.numpy as jnp
from jax import lax

D = 1024
HEAD_COUNT = 8
HEAD = 128
BLOCK = 64
DOCS = 4
SEQUENCE_TOKENS = 8192


def draw_decay_log(key, part):
    every_key_row = jax.random.split(key, 6)
    slow_share = 0.5
    slow_heads = jax.random.uniform(every_key_row[0], (HEAD_COUNT,)) < slow_share
    slow_rate = jnp.exp(jax.random.uniform(every_key_row[1], (HEAD_COUNT,), minval=math.log(0.2), maxval=math.log(0.8))) / SEQUENCE_TOKENS
    fast_rate = jnp.exp(jax.random.uniform(every_key_row[2], (HEAD_COUNT,), minval=math.log(1.0 / 50.0), maxval=math.log(1.0 / 30.0)))
    baseline_decay_rate = jnp.where(slow_heads, slow_rate, fast_rate)
    random_noise = jnp.exp(jax.random.uniform(every_key_row[3], (SEQUENCE_TOKENS, HEAD_COUNT), minval=-0.7, maxval=0.7))
    spike_locations = jax.random.uniform(every_key_row[4], (SEQUENCE_TOKENS, HEAD_COUNT)) < 3.0 / SEQUENCE_TOKENS
    spike_magnitude = jax.random.uniform(every_key_row[5], (SEQUENCE_TOKENS, HEAD_COUNT), minval=0.22, maxval=0.69)
    spike_values = jnp.where(spike_locations, spike_magnitude, 0.0)
    return (-(baseline_decay_rate[None, :] * random_noise + spike_values)).astype(jnp.float32)


def draw_doc_starts(key, part):
    last_block = SEQUENCE_TOKENS // BLOCK - 1
    starts_middle = jax.random.randint(key, (DOCS - 2,), 1, last_block)
    sorted_middle = jnp.sort(starts_middle).astype(jnp.int32) * BLOCK
    first_start = jnp.zeros((1,), jnp.int32)
    final_start = jnp.full((1,), last_block * BLOCK, jnp.int32)
    return jnp.concatenate([first_start, sorted_middle, final_start]).astype(jnp.int32)


def block_scale(key, shape, pieces, low, largest):
    loudness, own = 1.0, jax.random.fold_in(key, 6)
    for axis_at, blocks in pieces:
        draws = jnp.exp(jax.random.uniform(jax.random.fold_in(own, axis_at), (blocks,), jnp.float32, low / len(pieces), largest / len(pieces)))
        loudness = loudness * jnp.repeat(draws, shape[axis_at] // blocks).reshape([-1 if axis == axis_at else 1 for axis in range(len(shape))])
    return loudness


def scatter_about(key, extent, spread, limit, pieces=(), kind=jnp.bfloat16):
    array = spread * jax.random.normal(key, extent, jnp.float32)
    if pieces:
        array = array * block_scale(key, extent, pieces, -0.22, 0.18)
    return jnp.clip(array, -limit, limit).astype(kind)


def setup_inputs(seed: int = 0, part: int = 0) -> dict:
    arg_keys = jax.random.split(jax.random.key(seed), 8)
    own_keys = jax.random.split(jax.random.fold_in(arg_keys[7], part), 8)
    hidden = scatter_about(own_keys[0], (SEQUENCE_TOKENS, D), 1.0, 6.0, ((0, 16),))
    query_weight = scatter_about(arg_keys[1], (D, D), D ** -0.5, 0.1875)
    key_weight = scatter_about(arg_keys[2], (D, D), D ** -0.5, 0.1875)
    value_weight = scatter_about(arg_keys[3], (D, D), D ** -0.5, 0.1875)
    output_weight = scatter_about(arg_keys[4], (D, D), D ** -0.5, 0.1875)
    decay_log = draw_decay_log(jax.random.fold_in(jax.random.fold_in(arg_keys[7], part), 71), part)
    doc_starts = draw_doc_starts(jax.random.fold_in(jax.random.fold_in(arg_keys[7], part), 71), part)
    return dict(hidden=hidden, query_weight=query_weight, key_weight=key_weight, value_weight=value_weight, output_weight=output_weight, decay_log=decay_log, doc_starts=doc_starts)


def reference(hidden, query_weight, key_weight, value_weight, output_weight, decay_log, doc_starts):
    blocks = SEQUENCE_TOKENS // BLOCK
    block_rows = hidden.reshape(blocks, BLOCK, D)
    block_logs = decay_log.reshape(blocks, BLOCK, HEAD_COUNT)
    positions = jnp.arange(blocks, dtype=jnp.int32) * BLOCK
    resets = jnp.any(positions[:, None] == doc_starts[None, :].astype(jnp.int32), axis=1)
    keeps = jnp.where(resets, 0.0, 1.0).astype(jnp.float32)
    lower_mask = jnp.arange(BLOCK)[:, None] >= jnp.arange(BLOCK)[None, :]

    def step_block(state_now, inputs):
        row_block, log_block, keep_flag = inputs
        queries = jnp.dot(row_block, query_weight, preferred_element_type=jnp.float32).astype(jnp.bfloat16).reshape(BLOCK, HEAD_COUNT, HEAD)
        key_rows = jnp.dot(row_block, key_weight, preferred_element_type=jnp.float32).astype(jnp.bfloat16).reshape(BLOCK, HEAD_COUNT, HEAD)
        value_rows = jnp.dot(row_block, value_weight, preferred_element_type=jnp.float32).astype(jnp.bfloat16).reshape(BLOCK, HEAD_COUNT, HEAD)
        cumulative = jnp.cumsum(log_block, axis=0)
        state_now = state_now * keep_flag
        scores = jnp.einsum('jhd,ihd->hji', queries.astype(jnp.float32), key_rows.astype(jnp.float32))
        cum_heads = cumulative.T
        gap_matrix = cum_heads[:, :, None] - cum_heads[:, None, :]
        weights = (jnp.where(lower_mask[None], jnp.exp(gap_matrix), 0.0) * scores).astype(jnp.bfloat16)
        intra_term = jnp.einsum('hji,ihd->jhd', weights.astype(jnp.float32), value_rows.astype(jnp.float32))
        inter_term = jnp.einsum('jhd,hde->jhe', queries.astype(jnp.float32), state_now, precision=lax.Precision.HIGHEST) * jnp.exp(cumulative)[:, :, None]
        attended = intra_term + inter_term
        scaled = key_rows.astype(jnp.float32) * jnp.exp(cumulative[-1][None, :] - cumulative)[:, :, None]
        state_next = state_now * jnp.exp(cumulative[-1])[:, None, None] + jnp.einsum('ihd,ihe->hde', scaled, value_rows.astype(jnp.float32), precision=lax.Precision.HIGHEST)
        normed = attended * lax.rsqrt(lax.optimization_barrier(jnp.mean(attended * attended, axis=2, keepdims=True)) + 1e-06)
        normed = normed.astype(jnp.bfloat16).reshape(BLOCK, D)
        return (state_next, jnp.dot(normed, output_weight, preferred_element_type=jnp.float32).astype(jnp.bfloat16))
    initial = jnp.zeros((HEAD_COUNT, HEAD, HEAD), jnp.float32)
    _, outputs = lax.scan(step_block, initial, (block_rows, block_logs, keeps))
    return outputs.reshape(SEQUENCE_TOKENS, D)
```

```python
import functools

import jax
import jax.numpy as jnp
from jax import lax
from jax.experimental import pallas as pl
from jax.experimental.pallas import tpu as pltpu
from jax.sharding import PartitionSpec as P

D = 1024
HEAD_COUNT = 8
HEAD = 128
BLOCK = 64
PAIRS = HEAD_COUNT // 2
WIDE = 2 * HEAD
SPLIT = 1
ROWS = HEAD // SPLIT
CHUNKS = PAIRS * SPLIT
F32 = jnp.float32
BF16 = jnp.bfloat16
MESH = pl.DeviceIdType.MESH
RESET = -128.0


def dot(a, b):
    return jnp.dot(a, b, preferred_element_type=F32)


def kernel(outer, inner, tok, hidden_hbm, wq_hbm, wk_hbm, wv_hbm, wo_hbm, decay_hbm, docs_ref, out_ref,
           hid, wq, wk, wv, wo, dec, cum_s, cumt_s, q_s, k_s, v_s, qg_s, att_s, acc_s, w_s, grow_s,
           own, other, zin, zout, yin, yout, mout, sin, gbuf, fac,
           load_sem, g_send, g_recv, m1_send, m1_recv, z_send, z_recv, y_send, y_recv, m4_send, m4_recv):
    me = lax.axis_index("ctx")
    group = lax.axis_index("groups")
    core = lax.rem(me, 2)
    b = lax.rem(me // 2, inner)
    a = me // (2 * inner)
    slot = b * 2 + core
    plane = 2 * inner

    def at(aa, bb, cc):
        return (group, (aa * inner + bb) * 2 + cc)

    def peer(o):
        return lax.rem(slot + o, plane)

    loads = []

    def load(src, dst):
        c = pltpu.make_async_copy(src, dst, load_sem.at[len(loads)])
        c.start()
        loads.append(c)
        return c

    barrier = pltpu.get_barrier_semaphore()
    for o in range(1, plane):
        pl.semaphore_signal(barrier, inc=1, device_id=(group, a * plane + peer(o)), device_id_type=MESH)

    @pl.when(a > 0)
    def _():
        pl.semaphore_signal(barrier, inc=1, device_id=at(a - 1, b, core), device_id_type=MESH)

    @pl.when(a < outer - 1)
    def _():
        pl.semaphore_signal(barrier, inc=1, device_id=at(a + 1, b, core), device_id_type=MESH)

    ld_dec = load(decay_hbm, dec)
    ld_hid = load(hidden_hbm, hid)
    ld_kv = []
    for p in range(PAIRS):
        cols = pl.ds(p * WIDE, WIDE)
        ld_kv.append((load(wk_hbm.at[:, cols], wk.at[p]), load(wv_hbm.at[:, cols], wv.at[p])))
    ld_q = load(wq_hbm, wq)
    ld_o = load(wo_hbm, wo)

    row = lax.broadcasted_iota(jnp.int32, (tok, tok), 0)
    col = lax.broadcasted_iota(jnp.int32, (tok, tok), 1)
    lower = jnp.where(row >= col, 1.0, 0.0).astype(BF16)
    place = me * tok + lax.broadcasted_iota(jnp.int32, (tok, HEAD_COUNT), 0)
    hit = place == docs_ref[0]
    for i in range(1, docs_ref.shape[0]):
        hit = hit | (place == docs_ref[i])
    ld_dec.wait()
    cum_s[...] = jnp.zeros_like(cum_s)
    cum_s[:, 0:HEAD_COUNT] = dec[...] + jnp.where(hit, RESET, 0.0)
    full = cum_s[...]
    hi = full.astype(BF16)
    rest = full - hi.astype(F32)
    mid = rest.astype(BF16)
    low = (rest - mid.astype(F32)).astype(BF16)
    cum = dot(lower, hi) + (dot(lower, mid) + dot(lower, low))
    cum_s[...] = cum
    cumt = cum.T
    cumt_s[...] = cumt[0:HEAD_COUNT, :]
    w_s[...] = jnp.exp(cum[tok - 1:tok, :] - cum)
    grow_s[...] = jnp.exp(cum)
    gown = jnp.exp(jnp.broadcast_to(cumt[0:HEAD_COUNT, tok - 1:tok], (HEAD_COUNT, HEAD)))
    gbuf[pl.ds(slot, 1)] = gown[None]

    pl.semaphore_wait(barrier, plane - 1 + jnp.where(a > 0, 1, 0) + jnp.where(a < outer - 1, 1, 0))

    def g_copy(o):
        return pltpu.make_async_remote_copy(
            src_ref=gbuf.at[slot], dst_ref=gbuf.at[slot], send_sem=g_send.at[o], recv_sem=g_recv.at[slot],
            device_id=(group, a * plane + peer(o)), device_id_type=MESH)

    def g_land(o):
        s = peer(o)
        return pltpu.make_async_remote_copy(
            src_ref=gbuf.at[s], dst_ref=gbuf.at[s], send_sem=g_send.at[o], recv_sem=g_recv.at[s],
            device_id=(group, a * plane + peer(o)), device_id_type=MESH)

    for o in range(1, plane):
        g_copy(o).start()

    @pl.when(a == 0)
    def _():
        zin[...] = jnp.zeros_like(zin)
        for o in range(1, inner):
            bb = lax.rem(b + o, inner)

            @pl.when(bb > b)
            def _():
                for qq in range(CHUNKS):
                    yin[qq, pl.ds(bb, 1)] = jnp.zeros((1, ROWS, HEAD), F32)

    def head_of(p, c):
        return 2 * p + c

    def m1_copy(q):
        p, s = divmod(q, SPLIT)
        return pltpu.make_async_remote_copy(
            src_ref=own.at[head_of(p, 1 - core) * SPLIT + s], dst_ref=other.at[q],
            send_sem=m1_send.at[q], recv_sem=m1_recv.at[q], device_id=at(a, b, 1 - core), device_id_type=MESH)

    def z_copy(q):
        return pltpu.make_async_remote_copy(
            src_ref=zout.at[q], dst_ref=zin.at[q], send_sem=z_send.at[q], recv_sem=z_recv.at[q],
            device_id=at(jnp.minimum(a + 1, outer - 1), b, core), device_id_type=MESH)

    def y_copy(q, o, src):
        return pltpu.make_async_remote_copy(
            src_ref=src.at[q], dst_ref=yin.at[q, b], send_sem=y_send.at[q, o], recv_sem=y_recv.at[q, b],
            device_id=at(a, lax.rem(b + o, inner), core), device_id_type=MESH)

    def y_land(q, o):
        bb = lax.rem(b + o, inner)
        return pltpu.make_async_remote_copy(
            src_ref=yout.at[q], dst_ref=yin.at[q, bb], send_sem=y_send.at[q, o], recv_sem=y_recv.at[q, bb],
            device_id=at(a, bb, core), device_id_type=MESH)

    def m4_copy(q, c):
        p, s = divmod(q, SPLIT)
        return pltpu.make_async_remote_copy(
            src_ref=mout.at[q], dst_ref=sin.at[head_of(p, c) * SPLIT + s],
            send_sem=m4_send.at[q], recv_sem=m4_recv.at[q], device_id=at(a, b, 1 - core), device_id_type=MESH)

    def factor(k, q):
        return fac[k, pl.ds(head_of(q // SPLIT, core), 1), :]

    def mine(q):
        p, s = divmod(q, SPLIT)
        return own[head_of(p, core) * SPLIT + s]

    def factors():
        for o in range(1, plane):
            g_land(o).wait_recv()
        chip = [gbuf[2 * i] * gbuf[2 * i + 1] for i in range(inner)]
        one = jnp.ones_like(chip[0])
        every, post, pre, upto = one, one, one, one
        for i in range(inner):
            every = every * chip[i]
            post = post * jnp.where(i > b, chip[i], one)
            pre = pre * jnp.where(i < b, chip[i], one)
            upto = upto * jnp.where(i <= b, chip[i], one)
        fac[0], fac[1], fac[2], fac[3] = every, post, upto, pre
        fac[4] = gbuf[pl.ds(2 * b, 1)][0]
        fac[5] = gbuf[pl.ds(2 * b + 1, 1)][0]
        for j in range(inner):
            between = one
            for i in range(j + 1, inner):
                between = between * jnp.where(i < b, chip[i], one)
            fac[6 + j] = jnp.where(j < b, between, pre)

    def relay(q):
        m1_copy(q).wait_recv()

        @pl.when(a > 0)
        def _():
            z_copy(q).wait_recv()

        mn, ot, before = mine(q), other[q], zin[q]
        first = jnp.where(core == 0, mn, ot)
        second = jnp.where(core == 0, ot, mn)
        total = factor(5, q) * first + second
        zout[q] = factor(0, q) * before + factor(1, q) * total
        yout[q] = factor(2, q) * before + total

        @pl.when(a < outer - 1)
        def _():
            z_copy(q).start()

        for o in range(1, inner):
            bb = lax.rem(b + o, inner)

            @pl.when(bb > b)
            def _():
                y_copy(q, o, yout).start()

            @pl.when((bb < b) & (a > 0))
            def _():
                y_copy(q, o, zin).start()

    def merge(q):
        state = factor(3, q) * zin[q]
        for o in range(1, inner):
            bb = lax.rem(b + o, inner)

            @pl.when((bb < b) | (a > 0))
            def _():
                y_land(q, o).wait_recv()

            weight = fac[pl.ds(6 + bb, 1), pl.ds(head_of(q // SPLIT, core), 1), :][0]
            state = state + weight * yin[q, pl.ds(bb, 1)][0]
        first = jnp.where(core == 0, mine(q), other[q])
        late = factor(4, q) * state + first
        p, s = divmod(q, SPLIT)
        sin[pl.ds(head_of(p, core) * SPLIT + s, 1)] = jnp.where(core == 0, state, late)[None]
        mout[q] = jnp.where(core == 0, late, state)
        m4_copy(q, core).start()

    def keys_values(p):
        ld_kv[p][0].wait()
        kp = dot(hid[...], wk[p]).astype(BF16)
        k_s[p] = kp
        ld_kv[p][1].wait()
        vp = dot(hid[...], wv[p]).astype(BF16)
        v_s[p] = vp
        scale = jnp.concatenate(
            [jnp.broadcast_to(w_s[:, 2 * p + i:2 * p + i + 1], (tok, HEAD)) for i in range(2)], axis=1)
        scaled = (kp.astype(F32) * scale).astype(BF16)
        both = lax.dot_general(scaled, vp, (((0,), (0,)), ((), ())), preferred_element_type=F32)
        for i in range(2):
            for s in range(SPLIT):
                own[(2 * p + i) * SPLIT + s] = both[i * HEAD + s * ROWS:i * HEAD + (s + 1) * ROWS,
                                                    i * HEAD:(i + 1) * HEAD]
        for s in range(SPLIT):
            m1_copy(p * SPLIT + s).start()

    def query(p):
        qp = dot(hid[...], wq[:, p * WIDE:(p + 1) * WIDE]).astype(BF16)
        q_s[p] = qp
        scale = jnp.concatenate(
            [jnp.broadcast_to(grow_s[:, 2 * p + i:2 * p + i + 1], (tok, HEAD)) for i in range(2)], axis=1)
        qg_s[p] = (qp.astype(F32) * scale).astype(BF16)

    half = tok // 2
    tri = (lax.broadcasted_iota(jnp.int32, (half, half), 0) >= lax.broadcasted_iota(jnp.int32, (half, half), 1))

    def inside(h):
        p, i = divmod(h, 2)
        lanes = slice(i * HEAD, (i + 1) * HEAD)
        for r in range(2):
            rows = slice(r * half, (r + 1) * half)
            qh = q_s[p, rows, lanes]
            cj = cum_s[rows, h:h + 1]
            total = None
            for c in range(r + 1):
                cols = slice(c * half, (c + 1) * half)
                score = lax.dot_general(qh, k_s[p, cols, lanes], (((1,), (1,)), ((), ())),
                                        preferred_element_type=F32)
                fade = jnp.exp(cj - cumt_s[h:h + 1, cols])
                if c == r:
                    fade = jnp.where(tri, fade, 0.0)
                part = dot((fade * score).astype(BF16), v_s[p, cols, lanes])
                total = part if total is None else total + part
            att_s[rows, h * HEAD:(h + 1) * HEAD] = total

    def finish(p):
        for s in range(SPLIT):
            m4_copy(p * SPLIT + s, 1 - core).wait_recv()
        halves = []
        for i in range(2):
            h = 2 * p + i
            lanes = slice(i * HEAD, (i + 1) * HEAD)
            state = jnp.concatenate([sin[h * SPLIT + s] for s in range(SPLIT)], axis=0) if SPLIT > 1 else sin[h]
            att = att_s[:, h * HEAD:(h + 1) * HEAD] + dot(qg_s[p, :, lanes], state.astype(BF16))
            norm = lax.rsqrt(jnp.mean(att * att, axis=1, keepdims=True) + 1e-06)
            halves.append((att * norm).astype(BF16))
        normed = jnp.concatenate(halves, axis=1)
        part = dot(normed, wo[p * WIDE:(p + 1) * WIDE, :])
        if p == 0:
            acc_s[...] = part
        elif p < PAIRS - 1:
            acc_s[...] += part
        else:
            out_ref[...] = (acc_s[...] + part).astype(BF16)

    ld_hid.wait()
    for p in range(PAIRS):
        keys_values(p)
        if p == 0:
            factors()
        else:
            @pl.when(a == 0)
            def _():
                for s in range(SPLIT):
                    relay((p - 1) * SPLIT + s)
    ld_q.wait()
    work = [functools.partial(query, p) for p in range(PAIRS)] + [functools.partial(inside, h) for h in range(HEAD_COUNT)]
    plan = {(0, PAIRS - 1): 0, (1, 0): 2, (1, 1): 5, (1, 2): 8, (2, 0): 8}
    for u, unit in enumerate(work):
        unit()
        for (aa, p), when in plan.items():
            if when == u:
                @pl.when(a == aa)
                def _():
                    for s in range(SPLIT):
                        relay(p * SPLIT + s)

    def late_relay(p):
        early = [aa for (aa, pp) in plan if pp == p] + [0]
        cond = a > max(early)

        @pl.when(cond)
        def _():
            for s in range(SPLIT):
                relay(p * SPLIT + s)

    def merges(p):
        for s in range(SPLIT):
            merge(p * SPLIT + s)

    ld_o.wait()
    late_relay(0)
    late_relay(1)
    merges(0)
    late_relay(2)
    merges(1)
    finish(0)
    late_relay(3)
    merges(2)
    finish(1)
    merges(3)
    finish(2)
    finish(3)

    for o in range(1, plane):
        g_copy(o).wait_send()
    for q in range(CHUNKS):
        m1_copy(q).wait_send()
        m4_copy(q, core).wait_send()

        @pl.when(a < outer - 1)
        def _():
            z_copy(q).wait_send()

        for o in range(1, inner):
            bb = lax.rem(b + o, inner)

            @pl.when((bb > b) | (a > 0))
            def _():
                y_copy(q, o, yout).wait_send()


def body(outer, inner, hidden, query_weight, key_weight, value_weight, output_weight, decay_log, doc_starts):
    tok = hidden.shape[0]
    plane = 2 * inner
    state = (ROWS, HEAD)
    scratch = [
        pltpu.VMEM((tok, D), BF16),
        pltpu.VMEM((D, D), BF16),
        pltpu.VMEM((PAIRS, D, WIDE), BF16),
        pltpu.VMEM((PAIRS, D, WIDE), BF16),
        pltpu.VMEM((D, D), BF16),
        pltpu.VMEM((tok, HEAD_COUNT), F32),
        pltpu.VMEM((tok, HEAD), F32),
        pltpu.VMEM((HEAD_COUNT, tok), F32),
        pltpu.VMEM((PAIRS, tok, WIDE), BF16),
        pltpu.VMEM((PAIRS, tok, WIDE), BF16),
        pltpu.VMEM((PAIRS, tok, WIDE), BF16),
        pltpu.VMEM((PAIRS, tok, WIDE), BF16),
        pltpu.VMEM((tok, D), F32),
        pltpu.VMEM((tok, D), F32),
        pltpu.VMEM((tok, HEAD), F32),
        pltpu.VMEM((tok, HEAD), F32),
        pltpu.VMEM((HEAD_COUNT * SPLIT,) + state, F32),
        pltpu.VMEM((CHUNKS,) + state, F32),
        pltpu.VMEM((CHUNKS,) + state, F32),
        pltpu.VMEM((CHUNKS,) + state, F32),
        pltpu.VMEM((CHUNKS, inner) + state, F32),
        pltpu.VMEM((CHUNKS,) + state, F32),
        pltpu.VMEM((CHUNKS,) + state, F32),
        pltpu.VMEM((HEAD_COUNT * SPLIT,) + state, F32),
        pltpu.VMEM((plane, HEAD_COUNT, HEAD), F32),
        pltpu.VMEM((6 + inner, HEAD_COUNT, HEAD), F32),
        pltpu.SemaphoreType.DMA((4 + 2 * PAIRS,)),
        pltpu.SemaphoreType.DMA((plane,)),
        pltpu.SemaphoreType.DMA((plane,)),
        pltpu.SemaphoreType.DMA((CHUNKS,)),
        pltpu.SemaphoreType.DMA((CHUNKS,)),
        pltpu.SemaphoreType.DMA((CHUNKS,)),
        pltpu.SemaphoreType.DMA((CHUNKS,)),
        pltpu.SemaphoreType.DMA((CHUNKS, inner)),
        pltpu.SemaphoreType.DMA((CHUNKS, inner)),
        pltpu.SemaphoreType.DMA((CHUNKS,)),
        pltpu.SemaphoreType.DMA((CHUNKS,)),
    ]
    hbm = pl.BlockSpec(memory_space=pl.ANY)
    return pl.pallas_call(
        functools.partial(kernel, outer, inner, tok),
        out_shape=jax.ShapeDtypeStruct((tok, D), BF16),
        in_specs=[hbm] * 6 + [pl.BlockSpec(memory_space=pltpu.SMEM)],
        out_specs=pl.BlockSpec(memory_space=pltpu.VMEM),
        scratch_shapes=scratch,
        compiler_params=pltpu.CompilerParams(collective_id=0, has_side_effects=True,
                                             vmem_limit_bytes=50 * 1024 * 1024),
        name="decayed_layer",
    )(hidden, query_weight, key_weight, value_weight, output_weight, decay_log, doc_starts)


def solution(mesh):
    chips = mesh.shape["ctx"] // 2
    inner = 1
    while inner * inner * 4 <= chips:
        inner *= 2
    inner = max(inner, 1)
    outer = chips // inner
    spread = P(("groups", "ctx"), None)
    in_specs = (spread, P(), P(), P(), P(), spread, P("groups"))
    return jax.shard_map(functools.partial(body, outer, inner), mesh=mesh, in_specs=in_specs,
                         out_specs=spread, check_vma=False)
```

```python
import functools

import jax
import jax.numpy as jnp
from jax import lax
from jax.experimental import pallas as pl
from jax.experimental.pallas import tpu as pltpu
from jax.sharding import PartitionSpec as P

D = 1024
HEAD_COUNT = 8
HEAD = 128
BLOCK = 64
PAIRS = HEAD_COUNT // 2
WIDE = 2 * HEAD
SPLIT = 2
ROWS = HEAD // SPLIT
CHUNKS = PAIRS * SPLIT
F32 = jnp.float32
BF16 = jnp.bfloat16
MESH = pl.DeviceIdType.MESH
RESET = -128.0


def dot(a, b):
    return jnp.dot(a, b, preferred_element_type=F32)


def kernel(outer, inner, tok, hidden_hbm, wq_hbm, wk_hbm, wv_hbm, wo_hbm, decay_hbm, docs_hbm, out_ref,
           hid, wq, wk, wv, wo, dec, docs, cum_s, cumt_s, q_s, k_s, v_s, qg_s, att_s, acc_s, w_s, grow_s,
           own, other, zin, zout, yin, yout, mout, sin, gbuf, fac,
           load_sem, g_send, g_recv, m1_send, m1_recv, z_send, z_recv, y_send, y_recv, m4_send, m4_recv):
    me = lax.axis_index("ctx")
    group = lax.axis_index("groups")
    core = lax.rem(me, 2)
    b = lax.rem(me // 2, inner)
    a = me // (2 * inner)
    slot = b * 2 + core
    plane = 2 * inner

    def at(aa, bb, cc):
        return (group, (aa * inner + bb) * 2 + cc)

    def peer(o):
        return lax.rem(slot + o, plane)

    loads = []

    def load(src, dst):
        c = pltpu.make_async_copy(src, dst, load_sem.at[len(loads)])
        c.start()
        loads.append(c)
        return c

    barrier = pltpu.get_barrier_semaphore()
    for o in range(1, plane):
        pl.semaphore_signal(barrier, inc=1, device_id=(group, a * plane + peer(o)), device_id_type=MESH)

    @pl.when(a > 0)
    def _():
        pl.semaphore_signal(barrier, inc=1, device_id=at(a - 1, b, core), device_id_type=MESH)

    @pl.when(a < outer - 1)
    def _():
        pl.semaphore_signal(barrier, inc=1, device_id=at(a + 1, b, core), device_id_type=MESH)

    ld_docs = load(docs_hbm, docs)
    ld_dec = load(decay_hbm, dec)
    ld_hid = load(hidden_hbm, hid)
    ld_kv = []
    for p in range(PAIRS):
        cols = pl.ds(p * WIDE, WIDE)
        ld_kv.append((load(wk_hbm.at[:, cols], wk.at[p]), load(wv_hbm.at[:, cols], wv.at[p])))
    ld_q = load(wq_hbm, wq)
    ld_o = load(wo_hbm, wo)

    row = lax.broadcasted_iota(jnp.int32, (tok, tok), 0)
    col = lax.broadcasted_iota(jnp.int32, (tok, tok), 1)
    upper = jnp.where(row <= col, 1.0, 0.0).astype(BF16)
    place = me * tok + lax.broadcasted_iota(jnp.int32, (HEAD_COUNT, tok), 1)
    ld_docs.wait()
    hit = place == docs[0]
    for i in range(1, docs.shape[0]):
        hit = hit | (place == docs[i])
    ld_dec.wait()
    full = dec[...] + jnp.where(hit, RESET, 0.0)
    hi = full.astype(BF16).astype(F32)
    rest = full - hi
    mid = rest.astype(BF16).astype(F32)
    parts = dot(jnp.concatenate([hi, mid, rest - mid], axis=0).astype(BF16), upper)
    n = HEAD_COUNT
    cumt = parts[0:n] + (parts[n:2 * n] + parts[2 * n:3 * n])
    cumt_s[...] = cumt
    cum = jnp.concatenate([cumt, jnp.zeros((HEAD - n, tok), F32)], axis=0).T
    cum_s[...] = cum
    w_s[...] = jnp.exp(cum[tok - 1:tok, :] - cum)
    grow_s[...] = jnp.exp(cum)
    gown = jnp.exp(jnp.broadcast_to(cumt[:, tok - 1:tok], (HEAD_COUNT, HEAD)))
    gbuf[pl.ds(slot, 1)] = gown[None]

    def g_copy(o):
        return pltpu.make_async_remote_copy(
            src_ref=gbuf.at[slot], dst_ref=gbuf.at[slot], send_sem=g_send.at[o], recv_sem=g_recv.at[slot],
            device_id=(group, a * plane + peer(o)), device_id_type=MESH)

    def g_land(o):
        s = peer(o)
        return pltpu.make_async_remote_copy(
            src_ref=gbuf.at[s], dst_ref=gbuf.at[s], send_sem=g_send.at[o], recv_sem=g_recv.at[s],
            device_id=(group, a * plane + peer(o)), device_id_type=MESH)

    @pl.when(a == 0)
    def _():
        zin[...] = jnp.zeros_like(zin)
        for o in range(1, inner):
            bb = lax.rem(b + o, inner)

            @pl.when(bb > b)
            def _():
                for qq in range(CHUNKS):
                    yin[qq, pl.ds(bb, 1)] = jnp.zeros((1, ROWS, HEAD), F32)

    def head_of(p, c):
        return 2 * p + c

    def m1_copy(q):
        p, s = divmod(q, SPLIT)
        return pltpu.make_async_remote_copy(
            src_ref=own.at[head_of(p, 1 - core) * SPLIT + s], dst_ref=other.at[q],
            send_sem=m1_send.at[q], recv_sem=m1_recv.at[q], device_id=at(a, b, 1 - core), device_id_type=MESH)

    def z_copy(q):
        return pltpu.make_async_remote_copy(
            src_ref=zout.at[q], dst_ref=zin.at[q], send_sem=z_send.at[q], recv_sem=z_recv.at[q],
            device_id=at(jnp.minimum(a + 1, outer - 1), b, core), device_id_type=MESH)

    def y_copy(q, o, src):
        return pltpu.make_async_remote_copy(
            src_ref=src.at[q], dst_ref=yin.at[q, b], send_sem=y_send.at[q, o], recv_sem=y_recv.at[q, b],
            device_id=at(a, lax.rem(b + o, inner), core), device_id_type=MESH)

    def y_land(q, o):
        bb = lax.rem(b + o, inner)
        return pltpu.make_async_remote_copy(
            src_ref=yout.at[q], dst_ref=yin.at[q, bb], send_sem=y_send.at[q, o], recv_sem=y_recv.at[q, bb],
            device_id=at(a, bb, core), device_id_type=MESH)

    def m4_copy(q, c):
        p, s = divmod(q, SPLIT)
        return pltpu.make_async_remote_copy(
            src_ref=mout.at[q], dst_ref=sin.at[head_of(p, c) * SPLIT + s],
            send_sem=m4_send.at[q], recv_sem=m4_recv.at[q], device_id=at(a, b, 1 - core), device_id_type=MESH)

    def factor(k, q):
        return fac[k, pl.ds(head_of(q // SPLIT, core), 1), :]

    def mine(q):
        p, s = divmod(q, SPLIT)
        return own[head_of(p, core) * SPLIT + s]

    def factors():
        for o in range(1, plane):
            g_land(o).wait_recv()
        chip = [gbuf[2 * i] * gbuf[2 * i + 1] for i in range(inner)]
        one = jnp.ones_like(chip[0])
        every, post, pre, upto = one, one, one, one
        for i in range(inner):
            every = every * chip[i]
            post = post * jnp.where(i > b, chip[i], one)
            pre = pre * jnp.where(i < b, chip[i], one)
            upto = upto * jnp.where(i <= b, chip[i], one)
        fac[0], fac[1], fac[2], fac[3] = every, post, upto, pre
        fac[4] = gbuf[pl.ds(2 * b, 1)][0]
        fac[5] = gbuf[pl.ds(2 * b + 1, 1)][0]
        for j in range(inner):
            between = one
            for i in range(j + 1, inner):
                between = between * jnp.where(i < b, chip[i], one)
            fac[6 + j] = jnp.where(j < b, between, pre)

    def relay(q):
        m1_copy(q).wait_recv()

        @pl.when(a > 0)
        def _():
            z_copy(q).wait_recv()

        mn, ot, before = mine(q), other[q], zin[q]
        first = jnp.where(core == 0, mn, ot)
        second = jnp.where(core == 0, ot, mn)
        total = factor(5, q) * first + second
        zout[q] = factor(0, q) * before + factor(1, q) * total
        yout[q] = factor(2, q) * before + total

        @pl.when(a < outer - 1)
        def _():
            z_copy(q).start()

        for o in range(1, inner):
            bb = lax.rem(b + o, inner)

            @pl.when(bb > b)
            def _():
                y_copy(q, o, yout).start()

            @pl.when((bb < b) & (a > 0))
            def _():
                y_copy(q, o, zin).start()

    def merge(q):
        state = factor(3, q) * zin[q]
        for o in range(1, inner):
            bb = lax.rem(b + o, inner)

            @pl.when((bb < b) | (a > 0))
            def _():
                y_land(q, o).wait_recv()

            weight = fac[pl.ds(6 + bb, 1), pl.ds(head_of(q // SPLIT, core), 1), :][0]
            state = state + weight * yin[q, pl.ds(bb, 1)][0]
        first = jnp.where(core == 0, mine(q), other[q])
        late = factor(4, q) * state + first
        p, s = divmod(q, SPLIT)
        sin[pl.ds(head_of(p, core) * SPLIT + s, 1)] = jnp.where(core == 0, state, late)[None]
        mout[q] = jnp.where(core == 0, late, state)
        m4_copy(q, core).start()

    def greet():
        pl.semaphore_wait(barrier, plane - 1 + jnp.where(a > 0, 1, 0) + jnp.where(a < outer - 1, 1, 0))
        for o in range(1, plane):
            g_copy(o).start()

    def keys_values(p):
        ld_kv[p][0].wait()
        kp = dot(hid[...], wk[p]).astype(BF16)
        k_s[p] = kp
        ld_kv[p][1].wait()
        vp = dot(hid[...], wv[p]).astype(BF16)
        v_s[p] = vp
        scale = jnp.concatenate(
            [jnp.broadcast_to(w_s[:, 2 * p + i:2 * p + i + 1], (tok, HEAD)) for i in range(2)], axis=1)
        scaled = (kp.astype(F32) * scale).astype(BF16)
        both = lax.dot_general(scaled, vp, (((0,), (0,)), ((), ())), preferred_element_type=F32)
        for i in range(2):
            for s in range(SPLIT):
                own[(2 * p + i) * SPLIT + s] = both[i * HEAD + s * ROWS:i * HEAD + (s + 1) * ROWS,
                                                    i * HEAD:(i + 1) * HEAD]
        if p == 0:
            greet()
        for s in range(SPLIT):
            m1_copy(p * SPLIT + s).start()

    def query(p):
        qp = dot(hid[...], wq[:, p * WIDE:(p + 1) * WIDE]).astype(BF16)
        q_s[p] = qp
        scale = jnp.concatenate(
            [jnp.broadcast_to(grow_s[:, 2 * p + i:2 * p + i + 1], (tok, HEAD)) for i in range(2)], axis=1)
        qg_s[p] = (qp.astype(F32) * scale).astype(BF16)

    half = tok // 2
    tri = (lax.broadcasted_iota(jnp.int32, (half, half), 0) >= lax.broadcasted_iota(jnp.int32, (half, half), 1))

    def inside(h):
        p, i = divmod(h, 2)
        lanes = slice(i * HEAD, (i + 1) * HEAD)
        for r in range(2):
            rows = slice(r * half, (r + 1) * half)
            qh = q_s[p, rows, lanes]
            cj = cum_s[rows, h:h + 1]
            total = None
            for c in range(r + 1):
                cols = slice(c * half, (c + 1) * half)
                score = lax.dot_general(qh, k_s[p, cols, lanes], (((1,), (1,)), ((), ())),
                                        preferred_element_type=F32)
                fade = jnp.exp(cj - cumt_s[h:h + 1, cols])
                if c == r:
                    fade = jnp.where(tri, fade, 0.0)
                part = dot((fade * score).astype(BF16), v_s[p, cols, lanes])
                total = part if total is None else total + part
            att_s[rows, h * HEAD:(h + 1) * HEAD] = total

    def finish(p):
        for s in range(SPLIT):
            m4_copy(p * SPLIT + s, 1 - core).wait_recv()
        halves = []
        for i in range(2):
            h = 2 * p + i
            lanes = slice(i * HEAD, (i + 1) * HEAD)
            state = jnp.concatenate([sin[h * SPLIT + s] for s in range(SPLIT)], axis=0) if SPLIT > 1 else sin[h]
            att = att_s[:, h * HEAD:(h + 1) * HEAD] + dot(qg_s[p, :, lanes], state.astype(BF16))
            norm = lax.rsqrt(jnp.mean(att * att, axis=1, keepdims=True) + 1e-06)
            halves.append((att * norm).astype(BF16))
        normed = jnp.concatenate(halves, axis=1)
        part = dot(normed, wo[p * WIDE:(p + 1) * WIDE, :])
        if p == 0:
            acc_s[...] = part
        elif p < PAIRS - 1:
            acc_s[...] += part
        else:
            out_ref[...] = (acc_s[...] + part).astype(BF16)

    ld_hid.wait()
    for p in range(PAIRS):
        keys_values(p)
        if p == 1:
            factors()
        if p > 0:
            @pl.when(a == 0)
            def _():
                for s in range(SPLIT):
                    relay((p - 1) * SPLIT + s)
    ld_q.wait()
    work = [functools.partial(query, p) for p in range(PAIRS)] + [functools.partial(inside, h) for h in range(HEAD_COUNT)]
    plan = {(0, 3): 0, (1, 0): 0, (1, 1): 2, (1, 2): 5, (1, 3): 6, (2, 0): 6, (2, 1): 8, (2, 2): 10, (2, 3): 11}
    for u, unit in enumerate(work):
        unit()
        for (aa, p), when in plan.items():
            if when == u:
                @pl.when(a == aa)
                def _():
                    for s in range(SPLIT):
                        relay(p * SPLIT + s)

    def late_relay(p):
        early = [aa for (aa, pp) in plan if pp == p] + [0]
        cond = a > max(early)

        @pl.when(cond)
        def _():
            for s in range(SPLIT):
                relay(p * SPLIT + s)

    def merges(p):
        for s in range(SPLIT):
            merge(p * SPLIT + s)

    ld_o.wait()
    late_relay(0)
    late_relay(1)
    merges(0)
    late_relay(2)
    merges(1)
    finish(0)
    late_relay(3)
    merges(2)
    finish(1)
    merges(3)
    finish(2)
    finish(3)

    for o in range(1, plane):
        g_copy(o).wait_send()
    for q in range(CHUNKS):
        m1_copy(q).wait_send()
        m4_copy(q, core).wait_send()

        @pl.when(a < outer - 1)
        def _():
            z_copy(q).wait_send()

        for o in range(1, inner):
            bb = lax.rem(b + o, inner)

            @pl.when((bb > b) | (a > 0))
            def _():
                y_copy(q, o, yout).wait_send()


def body(outer, inner, hidden, query_weight, key_weight, value_weight, output_weight, decay_log, doc_starts):
    tok = hidden.shape[0]
    plane = 2 * inner
    state = (ROWS, HEAD)
    scratch = [
        pltpu.VMEM((tok, D), BF16),
        pltpu.VMEM((D, D), BF16),
        pltpu.VMEM((PAIRS, D, WIDE), BF16),
        pltpu.VMEM((PAIRS, D, WIDE), BF16),
        pltpu.VMEM((D, D), BF16),
        pltpu.VMEM((HEAD_COUNT, tok), F32),
        pltpu.SMEM(doc_starts.shape, jnp.int32),
        pltpu.VMEM((tok, HEAD), F32),
        pltpu.VMEM((HEAD_COUNT, tok), F32),
        pltpu.VMEM((PAIRS, tok, WIDE), BF16),
        pltpu.VMEM((PAIRS, tok, WIDE), BF16),
        pltpu.VMEM((PAIRS, tok, WIDE), BF16),
        pltpu.VMEM((PAIRS, tok, WIDE), BF16),
        pltpu.VMEM((tok, D), F32),
        pltpu.VMEM((tok, D), F32),
        pltpu.VMEM((tok, HEAD), F32),
        pltpu.VMEM((tok, HEAD), F32),
        pltpu.VMEM((HEAD_COUNT * SPLIT,) + state, F32),
        pltpu.VMEM((CHUNKS,) + state, F32),
        pltpu.VMEM((CHUNKS,) + state, F32),
        pltpu.VMEM((CHUNKS,) + state, F32),
        pltpu.VMEM((CHUNKS, inner) + state, F32),
        pltpu.VMEM((CHUNKS,) + state, F32),
        pltpu.VMEM((CHUNKS,) + state, F32),
        pltpu.VMEM((HEAD_COUNT * SPLIT,) + state, F32),
        pltpu.VMEM((plane, HEAD_COUNT, HEAD), F32),
        pltpu.VMEM((6 + inner, HEAD_COUNT, HEAD), F32),
        pltpu.SemaphoreType.DMA((5 + 2 * PAIRS,)),
        pltpu.SemaphoreType.DMA((plane,)),
        pltpu.SemaphoreType.DMA((plane,)),
        pltpu.SemaphoreType.DMA((CHUNKS,)),
        pltpu.SemaphoreType.DMA((CHUNKS,)),
        pltpu.SemaphoreType.DMA((CHUNKS,)),
        pltpu.SemaphoreType.DMA((CHUNKS,)),
        pltpu.SemaphoreType.DMA((CHUNKS, inner)),
        pltpu.SemaphoreType.DMA((CHUNKS, inner)),
        pltpu.SemaphoreType.DMA((CHUNKS,)),
        pltpu.SemaphoreType.DMA((CHUNKS,)),
    ]
    hbm = pl.BlockSpec(memory_space=pltpu.HBM)
    return pl.pallas_call(
        functools.partial(kernel, outer, inner, tok),
        out_shape=jax.ShapeDtypeStruct((tok, D), BF16),
        in_specs=[hbm] * 7,
        out_specs=pl.BlockSpec(memory_space=pltpu.VMEM),
        scratch_shapes=scratch,
        compiler_params=pltpu.CompilerParams(collective_id=0, has_side_effects=True,
                                             vmem_limit_bytes=63 * 1024 * 1024),
        name="decayed_layer",
    )(hidden, query_weight, key_weight, value_weight, output_weight, decay_log.T, doc_starts)


def solution(mesh):
    chips = mesh.shape["ctx"] // 2
    inner = 1
    while inner * inner * 4 <= chips:
        inner *= 2
    inner = max(inner, 1)
    outer = chips // inner
    spread = P(("groups", "ctx"), None)
    in_specs = (spread, P(), P(), P(), P(), spread, P("groups"))
    return jax.shard_map(functools.partial(body, outer, inner), mesh=mesh, in_specs=in_specs,
                         out_specs=spread, check_vma=False)
```

```python
import functools

import jax
import jax.numpy as jnp
from jax import lax
from jax.experimental import pallas as pl
from jax.experimental.pallas import tpu as pltpu
from jax.sharding import PartitionSpec as P

D = 1024
HEAD_COUNT = 8
HEAD = 128
BLOCK = 64
PAIRS = HEAD_COUNT // 2
WIDE = 2 * HEAD
SPLIT = 2
ROWS = HEAD // SPLIT
CHUNKS = PAIRS * SPLIT
F32 = jnp.float32
BF16 = jnp.bfloat16
MESH = pl.DeviceIdType.MESH
RESET = -128.0


def dot(a, b):
    return jnp.dot(a, b, preferred_element_type=F32)


def kernel(outer, inner, tok, hidden_hbm, wq_hbm, wk_hbm, wv_hbm, wo_hbm, decay_hbm, docs_hbm, out_ref,
           hid, wq, wk, wv, wo, dec, docs, cum_s, cumt_s, q_s, k_s, v_s, qg_s, att_s, acc_s, w_s, grow_s,
           own, other, zin, zout, yin, yout, mout, sin, gbuf, fac,
           load_sem, g_send, g_recv, m1_send, m1_recv, z_send, z_recv, y_send, y_recv, m4_send, m4_recv):
    me = lax.axis_index("ctx")
    group = lax.axis_index("groups")
    core = lax.rem(me, 2)
    b = lax.rem(me // 2, inner)
    a = me // (2 * inner)
    slot = b * 2 + core
    plane = 2 * inner

    def at(aa, bb, cc):
        return (group, (aa * inner + bb) * 2 + cc)

    def peer(o):
        return lax.rem(slot + o, plane)

    loads = []

    def load(src, dst):
        c = pltpu.make_async_copy(src, dst, load_sem.at[len(loads)])
        c.start()
        loads.append(c)
        return c

    barrier = pltpu.get_barrier_semaphore()
    for o in range(1, plane):
        pl.semaphore_signal(barrier, inc=1, device_id=(group, a * plane + peer(o)), device_id_type=MESH)

    @pl.when(a > 0)
    def _():
        pl.semaphore_signal(barrier, inc=1, device_id=at(a - 1, b, core), device_id_type=MESH)

    @pl.when(a < outer - 1)
    def _():
        pl.semaphore_signal(barrier, inc=1, device_id=at(a + 1, b, core), device_id_type=MESH)

    ld_docs = load(docs_hbm, docs)
    ld_dec = load(decay_hbm, dec)
    ld_hid = load(hidden_hbm, hid)
    ld_kv = []
    for p in range(PAIRS):
        cols = pl.ds(p * WIDE, WIDE)
        ld_kv.append((load(wk_hbm.at[:, cols], wk.at[p]), load(wv_hbm.at[:, cols], wv.at[p])))
    ld_q = load(wq_hbm, wq)
    ld_o = load(wo_hbm, wo)

    row = lax.broadcasted_iota(jnp.int32, (tok, tok), 0)
    col = lax.broadcasted_iota(jnp.int32, (tok, tok), 1)
    upper = jnp.where(row <= col, 1.0, 0.0).astype(BF16)
    place = me * tok + lax.broadcasted_iota(jnp.int32, (HEAD_COUNT, tok), 1)
    ld_docs.wait()
    hit = place == docs[0]
    for i in range(1, docs.shape[0]):
        hit = hit | (place == docs[i])
    ld_dec.wait()
    full = dec[...] + jnp.where(hit, RESET, 0.0)
    hi = full.astype(BF16).astype(F32)
    rest = full - hi
    mid = rest.astype(BF16).astype(F32)
    parts = dot(jnp.concatenate([hi, mid, rest - mid], axis=0).astype(BF16), upper)
    n = HEAD_COUNT
    cumt = parts[0:n] + (parts[n:2 * n] + parts[2 * n:3 * n])
    cumt_s[...] = cumt
    cum = jnp.concatenate([cumt, jnp.zeros((HEAD - n, tok), F32)], axis=0).T
    cum_s[...] = cum
    w_s[...] = jnp.exp(cum[tok - 1:tok, :] - cum)
    grow_s[...] = jnp.exp(cum)
    gown = jnp.exp(jnp.broadcast_to(cumt[:, tok - 1:tok], (HEAD_COUNT, HEAD)))
    gbuf[pl.ds(slot, 1)] = gown[None]

    def g_copy(o):
        return pltpu.make_async_remote_copy(
            src_ref=gbuf.at[slot], dst_ref=gbuf.at[slot], send_sem=g_send.at[o], recv_sem=g_recv.at[slot],
            device_id=(group, a * plane + peer(o)), device_id_type=MESH)

    def g_land(o):
        s = peer(o)
        return pltpu.make_async_remote_copy(
            src_ref=gbuf.at[s], dst_ref=gbuf.at[s], send_sem=g_send.at[o], recv_sem=g_recv.at[s],
            device_id=(group, a * plane + peer(o)), device_id_type=MESH)

    @pl.when(a == 0)
    def _():
        zin[...] = jnp.zeros_like(zin)
        for o in range(1, inner):
            bb = lax.rem(b + o, inner)

            @pl.when(bb > b)
            def _():
                for qq in range(CHUNKS):
                    yin[qq, pl.ds(bb, 1)] = jnp.zeros((1, ROWS, HEAD), F32)

    def head_of(p, c):
        return 2 * p + c

    def m1_copy(q):
        p, s = divmod(q, SPLIT)
        return pltpu.make_async_remote_copy(
            src_ref=own.at[head_of(p, 1 - core) * SPLIT + s], dst_ref=other.at[q],
            send_sem=m1_send.at[q], recv_sem=m1_recv.at[q], device_id=at(a, b, 1 - core), device_id_type=MESH)

    def z_copy(q):
        return pltpu.make_async_remote_copy(
            src_ref=zout.at[q], dst_ref=zin.at[q], send_sem=z_send.at[q], recv_sem=z_recv.at[q],
            device_id=at(jnp.minimum(a + 1, outer - 1), b, core), device_id_type=MESH)

    def y_copy(q, o, src):
        return pltpu.make_async_remote_copy(
            src_ref=src.at[q], dst_ref=yin.at[q, b], send_sem=y_send.at[q, o], recv_sem=y_recv.at[q, b],
            device_id=at(a, lax.rem(b + o, inner), core), device_id_type=MESH)

    def y_land(q, o):
        bb = lax.rem(b + o, inner)
        return pltpu.make_async_remote_copy(
            src_ref=yout.at[q], dst_ref=yin.at[q, bb], send_sem=y_send.at[q, o], recv_sem=y_recv.at[q, bb],
            device_id=at(a, bb, core), device_id_type=MESH)

    def m4_copy(q, c):
        p, s = divmod(q, SPLIT)
        return pltpu.make_async_remote_copy(
            src_ref=mout.at[q], dst_ref=sin.at[head_of(p, c) * SPLIT + s],
            send_sem=m4_send.at[q], recv_sem=m4_recv.at[q], device_id=at(a, b, 1 - core), device_id_type=MESH)

    def factor(k, q):
        return fac[k, pl.ds(head_of(q // SPLIT, core), 1), :]

    def mine(q):
        p, s = divmod(q, SPLIT)
        return own[head_of(p, core) * SPLIT + s]

    def factors():
        for o in range(1, plane):
            g_land(o).wait_recv()
        chip = [gbuf[2 * i] * gbuf[2 * i + 1] for i in range(inner)]
        one = jnp.ones_like(chip[0])
        every, post, pre, upto = one, one, one, one
        for i in range(inner):
            every = every * chip[i]
            post = post * jnp.where(i > b, chip[i], one)
            pre = pre * jnp.where(i < b, chip[i], one)
            upto = upto * jnp.where(i <= b, chip[i], one)
        fac[0], fac[1], fac[2], fac[3] = every, post, upto, pre
        fac[4] = gbuf[pl.ds(2 * b, 1)][0]
        fac[5] = gbuf[pl.ds(2 * b + 1, 1)][0]
        for j in range(inner):
            between = one
            for i in range(j + 1, inner):
                between = between * jnp.where(i < b, chip[i], one)
            fac[6 + j] = jnp.where(j < b, between, pre)

    def relay(q):
        m1_copy(q).wait_recv()

        @pl.when(a > 0)
        def _():
            z_copy(q).wait_recv()

        mn, ot, before = mine(q), other[q], zin[q]
        first = jnp.where(core == 0, mn, ot)
        second = jnp.where(core == 0, ot, mn)
        total = factor(5, q) * first + second
        zout[q] = factor(0, q) * before + factor(1, q) * total
        yout[q] = factor(2, q) * before + total

        @pl.when(a < outer - 1)
        def _():
            z_copy(q).start()

        for o in range(1, inner):
            bb = lax.rem(b + o, inner)

            @pl.when(bb > b)
            def _():
                y_copy(q, o, yout).start()

            @pl.when((bb < b) & (a > 0))
            def _():
                y_copy(q, o, zin).start()

    def merge(q):
        state = factor(3, q) * zin[q]
        for o in range(1, inner):
            bb = lax.rem(b + o, inner)

            @pl.when((bb < b) | (a > 0))
            def _():
                y_land(q, o).wait_recv()

            weight = fac[pl.ds(6 + bb, 1), pl.ds(head_of(q // SPLIT, core), 1), :][0]
            state = state + weight * yin[q, pl.ds(bb, 1)][0]
        first = jnp.where(core == 0, mine(q), other[q])
        late = factor(4, q) * state + first
        p, s = divmod(q, SPLIT)
        sin[pl.ds(head_of(p, core) * SPLIT + s, 1)] = jnp.where(core == 0, state, late)[None]
        mout[q] = jnp.where(core == 0, late, state)
        m4_copy(q, core).start()

    def greet():
        pl.semaphore_wait(barrier, plane - 1 + jnp.where(a > 0, 1, 0) + jnp.where(a < outer - 1, 1, 0))
        for o in range(1, plane):
            g_copy(o).start()

    def keys_values(p):
        ld_kv[p][0].wait()
        kp = dot(hid[...], wk[p]).astype(BF16)
        k_s[p] = kp
        ld_kv[p][1].wait()
        vp = dot(hid[...], wv[p]).astype(BF16)
        v_s[p] = vp
        scale = jnp.concatenate(
            [jnp.broadcast_to(w_s[:, 2 * p + i:2 * p + i + 1], (tok, HEAD)) for i in range(2)], axis=1)
        scaled = (kp.astype(F32) * scale).astype(BF16)
        both = lax.dot_general(scaled, vp, (((0,), (0,)), ((), ())), preferred_element_type=F32)
        for i in range(2):
            for s in range(SPLIT):
                own[(2 * p + i) * SPLIT + s] = both[i * HEAD + s * ROWS:i * HEAD + (s + 1) * ROWS,
                                                    i * HEAD:(i + 1) * HEAD]
        if p == 0:
            greet()
        for s in range(SPLIT):
            m1_copy(p * SPLIT + s).start()

    def query(p):
        qp = dot(hid[...], wq[:, p * WIDE:(p + 1) * WIDE]).astype(BF16)
        q_s[p] = qp
        scale = jnp.concatenate(
            [jnp.broadcast_to(grow_s[:, 2 * p + i:2 * p + i + 1], (tok, HEAD)) for i in range(2)], axis=1)
        qg_s[p] = (qp.astype(F32) * scale).astype(BF16)

    half = tok // 2
    tri = (lax.broadcasted_iota(jnp.int32, (half, half), 0) >= lax.broadcasted_iota(jnp.int32, (half, half), 1))

    def inside(h):
        p, i = divmod(h, 2)
        lanes = slice(i * HEAD, (i + 1) * HEAD)
        for r in range(2):
            rows = slice(r * half, (r + 1) * half)
            qh = q_s[p, rows, lanes]
            cj = cum_s[rows, h:h + 1]
            total = None
            for c in range(r + 1):
                cols = slice(c * half, (c + 1) * half)
                score = lax.dot_general(qh, k_s[p, cols, lanes], (((1,), (1,)), ((), ())),
                                        preferred_element_type=F32)
                fade = jnp.exp(cj - cumt_s[h:h + 1, cols])
                if c == r:
                    fade = jnp.where(tri, fade, 0.0)
                part = dot((fade * score).astype(BF16), v_s[p, cols, lanes])
                total = part if total is None else total + part
            att_s[rows, h * HEAD:(h + 1) * HEAD] = total

    def finish(p):
        for s in range(SPLIT):
            m4_copy(p * SPLIT + s, 1 - core).wait_recv()
        halves = []
        for i in range(2):
            h = 2 * p + i
            lanes = slice(i * HEAD, (i + 1) * HEAD)
            state = jnp.concatenate([sin[h * SPLIT + s] for s in range(SPLIT)], axis=0) if SPLIT > 1 else sin[h]
            att = att_s[:, h * HEAD:(h + 1) * HEAD] + dot(qg_s[p, :, lanes], state.astype(BF16))
            norm = lax.rsqrt(jnp.mean(att * att, axis=1, keepdims=True) + 1e-06)
            halves.append((att * norm).astype(BF16))
        normed = jnp.concatenate(halves, axis=1)
        part = dot(normed, wo[p * WIDE:(p + 1) * WIDE, :])
        if p == 0:
            acc_s[...] = part
        elif p < PAIRS - 1:
            acc_s[...] += part
        else:
            out_ref[...] = (acc_s[...] + part).astype(BF16)

    ld_hid.wait()
    for p in range(PAIRS):
        keys_values(p)
        if p == 1:
            factors()
        if p > 0:
            @pl.when(a == 0)
            def _():
                for s in range(SPLIT):
                    relay((p - 1) * SPLIT + s)
    ld_q.wait()
    work = [functools.partial(query, p) for p in range(PAIRS)] + [functools.partial(inside, h) for h in range(HEAD_COUNT)]
    plan = {(0, 3): 0, (1, 0): 0, (1, 1): 2, (1, 2): 5, (1, 3): 6, (2, 0): 6, (2, 1): 8, (2, 2): 10, (2, 3): 11}
    for u, unit in enumerate(work):
        unit()
        for (aa, p), when in plan.items():
            if when == u:
                @pl.when(a == aa)
                def _():
                    for s in range(SPLIT):
                        relay(p * SPLIT + s)

    def late_relay(p):
        early = [aa for (aa, pp) in plan if pp == p] + [0]
        cond = a > max(early)

        @pl.when(cond)
        def _():
            for s in range(SPLIT):
                relay(p * SPLIT + s)

    def merges(p):
        for s in range(SPLIT):
            merge(p * SPLIT + s)

    ld_o.wait()
    late_relay(0)
    late_relay(1)
    merges(0)
    late_relay(2)
    merges(1)
    finish(0)
    late_relay(3)
    merges(2)
    finish(1)
    merges(3)
    finish(2)
    finish(3)

    for o in range(1, plane):
        g_copy(o).wait_send()
    for q in range(CHUNKS):
        m1_copy(q).wait_send()
        m4_copy(q, core).wait_send()

        @pl.when(a < outer - 1)
        def _():
            z_copy(q).wait_send()

        for o in range(1, inner):
            bb = lax.rem(b + o, inner)

            @pl.when((bb > b) | (a > 0))
            def _():
                y_copy(q, o, yout).wait_send()


def body(outer, inner, hidden, query_weight, key_weight, value_weight, output_weight, decay_log, doc_starts):
    tok = hidden.shape[0]
    plane = 2 * inner
    state = (ROWS, HEAD)
    scratch = [
        pltpu.VMEM((tok, D), BF16),
        pltpu.VMEM((D, D), BF16),
        pltpu.VMEM((PAIRS, D, WIDE), BF16),
        pltpu.VMEM((PAIRS, D, WIDE), BF16),
        pltpu.VMEM((D, D), BF16),
        pltpu.VMEM((HEAD_COUNT, tok), F32),
        pltpu.SMEM(doc_starts.shape, jnp.int32),
        pltpu.VMEM((tok, HEAD), F32),
        pltpu.VMEM((HEAD_COUNT, tok), F32),
        pltpu.VMEM((PAIRS, tok, WIDE), BF16),
        pltpu.VMEM((PAIRS, tok, WIDE), BF16),
        pltpu.VMEM((PAIRS, tok, WIDE), BF16),
        pltpu.VMEM((PAIRS, tok, WIDE), BF16),
        pltpu.VMEM((tok, D), F32),
        pltpu.VMEM((tok, D), F32),
        pltpu.VMEM((tok, HEAD), F32),
        pltpu.VMEM((tok, HEAD), F32),
        pltpu.VMEM((HEAD_COUNT * SPLIT,) + state, F32),
        pltpu.VMEM((CHUNKS,) + state, F32),
        pltpu.VMEM((CHUNKS,) + state, F32),
        pltpu.VMEM((CHUNKS,) + state, F32),
        pltpu.VMEM((CHUNKS, inner) + state, F32),
        pltpu.VMEM((CHUNKS,) + state, F32),
        pltpu.VMEM((CHUNKS,) + state, F32),
        pltpu.VMEM((HEAD_COUNT * SPLIT,) + state, F32),
        pltpu.VMEM((plane, HEAD_COUNT, HEAD), F32),
        pltpu.VMEM((6 + inner, HEAD_COUNT, HEAD), F32),
        pltpu.SemaphoreType.DMA((5 + 2 * PAIRS,)),
        pltpu.SemaphoreType.DMA((plane,)),
        pltpu.SemaphoreType.DMA((plane,)),
        pltpu.SemaphoreType.DMA((CHUNKS,)),
        pltpu.SemaphoreType.DMA((CHUNKS,)),
        pltpu.SemaphoreType.DMA((CHUNKS,)),
        pltpu.SemaphoreType.DMA((CHUNKS,)),
        pltpu.SemaphoreType.DMA((CHUNKS, inner)),
        pltpu.SemaphoreType.DMA((CHUNKS, inner)),
        pltpu.SemaphoreType.DMA((CHUNKS,)),
        pltpu.SemaphoreType.DMA((CHUNKS,)),
    ]
    hbm = pl.BlockSpec(memory_space=pltpu.HBM)
    return pl.pallas_call(
        functools.partial(kernel, outer, inner, tok),
        out_shape=jax.ShapeDtypeStruct((tok, D), BF16),
        in_specs=[hbm] * 7,
        out_specs=pl.BlockSpec(memory_space=pltpu.VMEM),
        scratch_shapes=scratch,
        compiler_params=pltpu.CompilerParams(collective_id=0, has_side_effects=True,
                                             vmem_limit_bytes=52 * 1024 * 1024),
        name="decayed_layer",
    )(hidden, query_weight, key_weight, value_weight, output_weight, decay_log.T, doc_starts)


def solution(mesh):
    chips = mesh.shape["ctx"] // 2
    inner = 1
    while inner * inner * 4 <= chips:
        inner *= 2
    inner = max(inner, 1)
    outer = chips // inner
    spread = P(("groups", "ctx"), None)
    in_specs = (spread, P(), P(), P(), P(), spread, P("groups"))
    return jax.shard_map(functools.partial(body, outer, inner), mesh=mesh, in_specs=in_specs,
                         out_specs=spread, check_vma=False)
```
